32 devices in a mesh: rows: 8 (over y, x, core), tok: 4 (over z).
Axes of the slice: x: 2, y: 2, z: 4, core: 2. Of those that a mesh axis runs over, the one named last changes fastest.
Arguments:
- pixels: bfloat16 [1024, 425, 512], P('rows', None, 'tok'), as said below
- scene_starts: int32 [4], replicated, may hold values from 0 to 960, as said below
- owners: int32 [256, 128], P('rows', 'tok'), may hold values from 0 to 7, as said below
- start_basis: float32 [425, 64], replicated, may hold values from -6 to 6
Outputs:
- tokens: bfloat16 [32768, 1024], P(('rows', 'tok'))
- noise_scores: bfloat16 [1024, 64, 512], P('rows', None, 'tok')
The draws below stay inside these ranges and needn't reach their ends.
Inputs may be any that keep to these rules, and one draw needn't show every extreme that they name: `scene_starts`: entry 0 is 0 and the entries rise strictly. `owners`: in each block of 32 x 128/4 patches every owner appears exactly 128 times. `pixels`: finite radiances; the scenes have a positive mean.
All inputs are finite; a program needn't handle non-finite values. Where the reference program divides by a largest or mean magnitude, that divisor is 1e-20 or more.
Results may differ from the reference program's by a relative error of at most 0.0068.
Values may be sent and summed in bfloat16 or wider, within the bound.
A program may use at most 192 MiB of HBM per device.

```python
import jax
import jax.numpy as jnp
from jax import lax

B = 425
K = 64
PS = 4
NS_ITERS = 10
SUB_ITERS = 2
NSCENES = 4
RDEV = 128
CDEV = 128
IMG_ROWS = 1024
COLS = 512
PR = 256
PC = 128
PATCHES = 32768
PER = 128
TOKLEN = 1024
N_ROWS = 8
N_TOK = 4


def draw_pixels(key, part):
    keys = jax.random.split(key, 7)
    half_rows = IMG_ROWS // 2
    shared = jax.random.normal(keys[0], (half_rows, B + 1, COLS), jnp.float32)
    speckle = jax.random.normal(keys[1], (IMG_ROWS, B + 1, COLS), jnp.float32)
    band_level = jax.random.uniform(keys[5], (B,), jnp.float32, 0.5, 2.0)
    shared = jnp.repeat(shared, 2, axis=0)
    signal_gain = jnp.exp(jax.random.uniform(keys[2], (B + 1,), jnp.float32, jnp.log(0.5), jnp.log(5.0)))
    noise_gain = jnp.exp(jax.random.uniform(keys[3], (B + 1,), jnp.float32, jnp.log(0.7), jnp.log(3.0)))
    raw = shared * signal_gain[None, :, None] + speckle * noise_gain[None, :, None]
    mixed = raw[:, :B, :] + 0.7 * raw[:, 1:, :]
    row_block = jnp.arange(IMG_ROWS, dtype=jnp.int32) // RDEV
    pairing = jax.random.permutation(keys[4], N_ROWS).astype(jnp.int32)
    band_slot = jnp.arange(B, dtype=jnp.int32) % N_ROWS
    boost = jnp.where(band_slot[None, :] == pairing[row_block][:, None], 4.0, 1.0)
    column_gain = jax.random.uniform(keys[6], (COLS,), jnp.float32, 0.6, 1.6)
    bright = 1.0 + 2.0 * jnp.arange(IMG_ROWS, dtype=jnp.float32) / jnp.float32(IMG_ROWS - 1)
    value = (mixed * boost[:, :, None] + band_level[None, :, None]) * column_gain[None, None, :]
    value = value * bright[:, None, None]
    return value.astype(jnp.bfloat16)


def draw_scene_starts(key, part):
    last_start = IMG_ROWS - RDEV // 2
    picked = jax.random.permutation(key, last_start - 1)[:NSCENES - 2] + 1
    picked = jnp.sort(picked.astype(jnp.int32))
    return jnp.concatenate([jnp.zeros((1,), jnp.int32), picked, jnp.full((1,), last_start, jnp.int32)])


def draw_owners(key, part):
    rows_per = RDEV // PS
    cols_per = CDEV // PS
    count = rows_per * cols_per
    base = jnp.arange(count, dtype=jnp.int32) % N_ROWS
    keys = jax.random.split(key, N_ROWS * N_TOK)
    shuffled = jax.vmap(lambda single: jax.random.permutation(single, base))(keys)
    shuffled = shuffled.reshape(N_ROWS, N_TOK, rows_per, cols_per).transpose(0, 2, 1, 3)
    return shuffled.reshape(PR, PC).astype(jnp.int32)


def gaussian(stream_key, shape, scale, most, kind=jnp.bfloat16):
    result = jax.random.normal(stream_key, shape, jnp.float32) * scale
    return jnp.minimum(jnp.maximum(result, -most), most).astype(kind)


def setup_inputs(seed: int = 0) -> dict:
    arg_keys = jax.random.split(jax.random.key(seed), 5)
    return {
        "pixels": draw_pixels(jax.random.fold_in(arg_keys[4], 71), 0),
        "scene_starts": draw_scene_starts(jax.random.fold_in(arg_keys[4], 71), 0),
        "owners": draw_owners(jax.random.fold_in(arg_keys[4], 71), 0),
        "start_basis": gaussian(arg_keys[3], (B, K), 1.0, 6.0, jnp.float32),
    }


def product(left, right):
    return jnp.dot(left, right, precision=lax.Precision.HIGHEST)

def whiten(noise_cov):
    width = noise_cov.shape[0]
    scale = jnp.max(lax.optimization_barrier(jnp.sum(jnp.abs(noise_cov), axis=1)))
    identity = jnp.eye(width, dtype=jnp.float32)
    upper = noise_cov / scale
    lower = identity
    for repeat in range(NS_ITERS):
        middle = 1.5 * identity - 0.5 * product(lower, upper)
        upper = product(upper, middle)
        lower = product(middle, lower)
    return lower / jnp.sqrt(scale)

def orthonormal(block):
    gram = product(block.T, block)
    factor = jnp.linalg.cholesky(gram)
    return lax.linalg.triangular_solve(factor, block, left_side=False, lower=True, transpose_a=True)

def reference(pixels, scene_starts, owners, start_basis):
    total_rows = IMG_ROWS
    row_index = jnp.arange(total_rows, dtype=jnp.int32)
    successor = row_index + 1
    starting = jnp.any(successor[:, None] == scene_starts[None, :], axis=1)
    valid = jnp.logical_and(successor < total_rows, jnp.logical_not(starting))
    following = jnp.concatenate([pixels[1:], jnp.zeros_like(pixels[:1])], axis=0)
    pixel_blocks = pixels.reshape(N_ROWS, RDEV, B, COLS)
    follow_blocks = following.reshape(N_ROWS, RDEV, B, COLS)
    valid_blocks = valid.reshape(N_ROWS, RDEV)

    def block_differ(block, ahead, keep):
        gap = block.astype(jnp.float32) - ahead.astype(jnp.float32)
        return jnp.where(keep[:, None, None], gap, 0.0).astype(jnp.bfloat16)

    def moments(items):
        block, ahead, keep = items
        differ = block_differ(block, ahead, keep).astype(jnp.float32)
        wide = block.astype(jnp.float32)
        noise_term = jnp.einsum('rbc,rec->be', differ, differ, precision=lax.Precision.HIGHEST)
        signal_term = jnp.einsum('rbc,rec->be', wide, wide, precision=lax.Precision.HIGHEST)
        return (noise_term, signal_term, lax.optimization_barrier(jnp.sum(wide, axis=(0, 2))))
    noise_terms, signal_terms, pixel_terms = lax.map(moments, (pixel_blocks, follow_blocks, valid_blocks))
    pixel_total = jnp.float32(IMG_ROWS * COLS)
    noise_cov = lax.optimization_barrier(jnp.sum(noise_terms, axis=0)) / jnp.float32(2 * (IMG_ROWS - NSCENES) * COLS)
    pixel_mean = lax.optimization_barrier(jnp.sum(pixel_terms, axis=0)) / pixel_total
    signal_cov = lax.optimization_barrier(jnp.sum(signal_terms, axis=0)) / pixel_total - pixel_mean[:, None] * pixel_mean[None, :]
    whitener = whiten(noise_cov)
    whitened = product(product(whitener, signal_cov), whitener)
    basis = orthonormal(start_basis)
    for repeat in range(SUB_ITERS):
        basis = orthonormal(product(whitened, basis))
    projector = product(whitener, basis).astype(jnp.bfloat16)
    wide_projector = projector.astype(jnp.float32)
    offset = product(pixel_mean, wide_projector)

    def project(items):
        block, ahead, keep = items
        differ = block_differ(block, ahead, keep).astype(jnp.float32)
        wide = block.astype(jnp.float32)
        comps = jnp.einsum('bk,rbc->rkc', wide_projector, wide, precision=lax.Precision.HIGHEST) - offset[None, :, None]
        scores = jnp.einsum('bk,rbc->rkc', wide_projector, differ, precision=lax.Precision.HIGHEST)
        return (comps.astype(jnp.bfloat16), scores.astype(jnp.bfloat16))
    comp_blocks, score_blocks = lax.map(project, (pixel_blocks, follow_blocks, valid_blocks))
    components = comp_blocks.reshape(IMG_ROWS, K, COLS)
    noise_scores = score_blocks.reshape(IMG_ROWS, K, COLS)
    patch_tokens = components.reshape(PR, PS, K, PC, PS).transpose(0, 3, 1, 4, 2).reshape(PR, PC, TOKLEN)
    rows_per = RDEV // PS
    cols_per = CDEV // PS
    block_tokens = patch_tokens.reshape(N_ROWS, rows_per, N_TOK, cols_per, TOKLEN).transpose(0, 2, 1, 3, 4)
    block_tokens = block_tokens.reshape(N_ROWS, N_TOK, rows_per * cols_per, TOKLEN)
    block_owners = owners.reshape(N_ROWS, rows_per, N_TOK, cols_per).transpose(0, 2, 1, 3)
    block_owners = block_owners.reshape(N_ROWS, N_TOK, rows_per * cols_per)
    order = jnp.argsort(block_owners, axis=-1, stable=True).astype(jnp.int32)
    ordered = jnp.take_along_axis(block_tokens, order[:, :, :, None], axis=2)
    ordered = ordered.reshape(N_ROWS, N_TOK, N_ROWS, PER, TOKLEN).transpose(2, 1, 0, 3, 4)
    tokens = ordered.reshape(PATCHES, TOKLEN)
    return (tokens, noise_scores)
```

```python
import functools

import jax
import jax.numpy as jnp
from jax import lax
from jax.experimental import pallas as pl
from jax.experimental.pallas import tpu as pltpu
from jax.sharding import PartitionSpec as P

PS = 4
NS_ITERS = 10
STEP = 16
HALF = 256
F32 = jnp.float32
BF16 = jnp.bfloat16
NT = (((1,), (1,)), ((), ()))


def up(value, unit):
    return -(-value // unit) * unit


def passed_along(value, axis, steps):
    count = lax.axis_size(axis)
    leading, last = (max(0, -steps), min(count, count - steps))
    return lax.ppermute(value, axis, [(source, source + steps) for source in range(leading, last)])


def moments_kernel(x_ref, ahead_ref, halo_ref, valid_ref, wide_ref, tail_ref, band_ref, xs, ds, total):
    step = pl.program_id(0)
    steps = pl.num_programs(0)
    rows, bands, cols = x_ref.shape
    tall = xs.shape[0]

    @pl.when(step == 0)
    def _():
        wide_ref[...] = jnp.zeros_like(wide_ref)
        tail_ref[...] = jnp.zeros_like(tail_ref)
        total[...] = jnp.zeros_like(total)
        xs[...] = jnp.zeros_like(xs)
        ds[...] = jnp.zeros_like(ds)

    last = step == steps - 1
    here = x_ref[0].astype(F32)
    sums = total[...]
    for r in range(rows):
        if r + 1 < rows:
            after = x_ref[r + 1].astype(F32)
        else:
            after = jnp.where(last, halo_ref[0], ahead_ref[0]).astype(F32)
        keep = valid_ref[step * rows + r] != 0
        at = slice(r * cols, (r + 1) * cols)
        xs[0:bands, at] = x_ref[r]
        ds[0:bands, at] = jnp.where(keep, here - after, 0.0).astype(BF16)
        sums = sums + here
        here = after
    total[...] = sums
    for index, ref in enumerate((ds, xs)):
        wide_ref[index] += lax.dot_general(
            ref[...], ref[0:HALF, :], NT, preferred_element_type=F32
        )
        tail_ref[index] += lax.dot_general(
            ref[HALF:tall, :], ref[HALF:tall, :], NT, preferred_element_type=F32
        )

    @pl.when(last)
    def _():
        band_ref[...] = jnp.zeros_like(band_ref)
        band_ref[0:bands, :] = jnp.sum(total[...], axis=1, keepdims=True)


def moments(pixels, halo, valid):
    local_rows, bands, cols = pixels.shape
    tall = up(bands, 16)
    steps = local_rows // STEP
    last_row = local_rows - 1
    return pl.pallas_call(
        moments_kernel,
        grid=(steps,),
        in_specs=[
            pl.BlockSpec((STEP, bands, cols), lambda i: (i, 0, 0)),
            pl.BlockSpec((1, bands, cols), lambda i: (jnp.minimum((i + 1) * STEP, last_row), 0, 0)),
            pl.BlockSpec((1, bands, cols), lambda i: (0, 0, 0)),
            pl.BlockSpec(memory_space=pltpu.SMEM),
        ],
        out_specs=[
            pl.BlockSpec((2, tall, HALF), lambda i: (0, 0, 0)),
            pl.BlockSpec((2, tall - HALF, tall - HALF), lambda i: (0, 0, 0)),
            pl.BlockSpec((tall, 1), lambda i: (0, 0)),
        ],
        out_shape=[
            jax.ShapeDtypeStruct((2, tall, HALF), F32),
            jax.ShapeDtypeStruct((2, tall - HALF, tall - HALF), F32),
            jax.ShapeDtypeStruct((tall, 1), F32),
        ],
        scratch_shapes=[
            pltpu.VMEM((tall, STEP * cols), BF16),
            pltpu.VMEM((tall, STEP * cols), BF16),
            pltpu.VMEM((bands, cols), F32),
        ],
        compiler_params=pltpu.CompilerParams(vmem_limit_bytes=48 * 2**20),
        cost_estimate=pl.CostEstimate(
            flops=4 * local_rows * cols * bands * bands,
            bytes_accessed=2 * local_rows * cols * bands,
            transcendentals=0,
        ),
        name="moments",
    )(pixels, pixels, halo, valid)


def split(value):
    high = value.astype(BF16)
    return high, (value - high.astype(F32)).astype(BF16)


def dot3(left, right):
    (lh, ll), (rh, rl) = left, right
    dot = functools.partial(jnp.dot, preferred_element_type=F32)
    return dot(lh, rh) + (dot(ll, rh) + dot(lh, rl))


def dot3_nt(left, right):
    (lh, ll), (rh, rl) = left, right
    dot = functools.partial(lax.dot_general, dimension_numbers=NT, preferred_element_type=F32)
    return dot(lh, rh) + (dot(ll, rh) + dot(lh, rl))


def projector_kernel(
    noise_norm, pixel_total, wide_ref, tail_ref, band_ref, start_ref, proj_ref, offset_ref,
    full, uh, ul, lh, ll, mh, ml, sh, sl,
):
    size = full.shape[0]
    tall = wide_ref.shape[1]
    bands = proj_ref.shape[1]
    comps = proj_ref.shape[0]
    rows = lax.broadcasted_iota(jnp.int32, (size, size), 0)
    lanes = lax.broadcasted_iota(jnp.int32, (size, size), 1)
    eye = jnp.where(rows == lanes, 1.0, 0.0).astype(F32)[0:tall]

    def assemble(index):
        full[...] = jnp.zeros_like(full)
        full[0:tall, 0:HALF] = wide_ref[index]
        full[HALF:tall, HALF:tall] = tail_ref[index]
        full[0:HALF, HALF:size] = full[HALF:size, 0:HALF].T
        return full[0:tall, :]

    def put(high, low, value):
        high[0:tall, :], low[0:tall, :] = split(value)

    for ref in (uh, ul, lh, ll, mh, ml, sh, sl):
        ref[...] = jnp.zeros_like(ref)
    band = jnp.broadcast_to(band_ref[...], (tall, 128)) / pixel_total
    band = jnp.concatenate([band, jnp.zeros((size - tall, 128), F32)], axis=0)
    mean_col = band[0:tall, 0:1]
    mean_row = band.T[0:1, :]
    put(sh, sl, assemble(1) / pixel_total - mean_col * mean_row)

    noise_cov = assemble(0) / noise_norm
    scale = jnp.max(jnp.sum(jnp.abs(noise_cov), axis=1, keepdims=True), axis=0, keepdims=True)
    upper = noise_cov / scale
    put(uh, ul, upper)
    middle = 1.5 * eye - 0.5 * upper
    put(mh, ml, middle)
    put(lh, ll, middle)

    def pair(high, low):
        return high[...], low[...]

    def left(high, low):
        return high[0:tall, :], low[0:tall, :]

    put(uh, ul, dot3(left(uh, ul), pair(mh, ml)))

    def iteration(repeat, carry):
        put(mh, ml, 1.5 * eye - 0.5 * dot3(left(lh, ll), pair(uh, ul)))
        put(uh, ul, dot3(left(uh, ul), pair(mh, ml)))
        put(lh, ll, dot3(left(lh, ll), pair(mh, ml)))
        return carry

    lax.fori_loop(0, NS_ITERS - 2, iteration, 0)
    put(mh, ml, 1.5 * eye - 0.5 * dot3(left(lh, ll), pair(uh, ul)))
    whitener = dot3(left(lh, ll), pair(mh, ml)) * lax.rsqrt(scale)
    put(lh, ll, whitener)

    def whitened(block):
        for high, low in ((lh, ll), (sh, sl), (lh, ll)):
            block = dot3(split(block), pair(high, low))
        return block

    block = whitened(start_ref[...])
    largest = jnp.max(jnp.max(jnp.abs(block), axis=1, keepdims=True), axis=0, keepdims=True)
    block = whitened(block / largest)
    largest = jnp.max(jnp.max(jnp.abs(block), axis=1, keepdims=True), axis=0, keepdims=True)
    block = block / largest
    gram = lax.dot_general(
        block, block, NT, precision=lax.Precision.HIGHEST, preferred_element_type=F32
    )
    k_rows = lax.broadcasted_iota(jnp.int32, (comps, comps), 0)
    k_lanes = lax.broadcasted_iota(jnp.int32, (comps, comps), 1)
    work = jnp.concatenate([gram, jnp.where(k_rows == k_lanes, 1.0, 0.0).astype(F32)], axis=1)
    row_index = lax.broadcasted_iota(jnp.int32, (comps, 2 * comps), 0)
    for j in range(comps):
        pivot_row = work[j:j + 1, :]
        inverse = lax.rsqrt(pivot_row[:, j:j + 1])
        pivot_row = pivot_row * inverse
        factor = work[:, j:j + 1] * inverse
        work = jnp.where(
            row_index > j, work - factor * pivot_row, jnp.where(row_index == j, pivot_row, work)
        )
    basis = jnp.dot(
        work[:, comps:], block, precision=lax.Precision.HIGHEST, preferred_element_type=F32
    )
    projector = dot3(split(basis), pair(lh, ll)).astype(BF16)
    proj_ref[...] = projector[:, 0:bands]
    offset = jnp.sum(projector.astype(F32) * mean_row, axis=1, keepdims=True)
    offset_ref[...] = jnp.broadcast_to(offset, offset_ref.shape)


def make_projector(wide, tail, band, start, noise_norm, pixel_total):
    tall = wide.shape[1]
    comps, size = start.shape[0], up(tall, 128)
    square = pltpu.VMEM((size, size), BF16)
    return pl.pallas_call(
        functools.partial(projector_kernel, noise_norm, pixel_total),
        out_shape=[
            jax.ShapeDtypeStruct((comps, tall), BF16),
            jax.ShapeDtypeStruct((comps, 128), F32),
        ],
        scratch_shapes=[pltpu.VMEM((size, size), F32)] + [square] * 8,
        compiler_params=pltpu.CompilerParams(vmem_limit_bytes=48 * 2**20),
        name="projector",
    )(wide, tail, band, jnp.pad(start, ((0, 0), (0, size - start.shape[1]))))


def project_kernel(
    x_ref, halo_ref, valid_ref, proj_ref, offset_ref, place_ref, spread_ref,
    tokens_ref, scores_ref, ahead, raster,
):
    step = pl.program_id(0)
    steps = pl.num_programs(0)
    block = steps - 1 - step
    rows, bands, cols = x_ref.shape
    comps = proj_ref.shape[0]
    projector = proj_ref[...][:, 0:bands]
    dot = functools.partial(jnp.dot, preferred_element_type=F32)

    @pl.when(step == 0)
    def _():
        ahead[...] = dot(projector, halo_ref[0])

    pixels = jnp.concatenate([x_ref[r] for r in range(rows)], axis=1)
    sums = dot(projector, pixels)
    offset = offset_ref[...]
    after = ahead[...]
    for r in reversed(range(rows)):
        here = sums[:, r * cols:(r + 1) * cols]
        keep = valid_ref[block * rows + r] != 0
        scores_ref[r] = jnp.where(keep, here - after, 0.0).astype(BF16)
        after = here
    ahead[...] = after

    patches = rows // PS
    groups = cols // PS
    chosen_row = lax.broadcasted_iota(jnp.int32, (cols, cols), 0)
    chosen_col = lax.broadcasted_iota(jnp.int32, (cols, cols), 1)
    chosen = jnp.where(
        chosen_col == PS * lax.rem(chosen_row, groups) + lax.div(chosen_row, groups), 1.0, 0.0
    ).astype(BF16)
    columns = []
    for p in range(patches):
        parts = []
        for i in range(PS):
            r = p * PS + i
            parts.append((sums[:, r * cols:(r + 1) * cols] - offset).astype(BF16))
        stacked = jnp.concatenate(parts, axis=0)
        columns.append(
            lax.dot_general(chosen, stacked, NT, preferred_element_type=F32).astype(BF16)
        )
    pair = 2 * comps
    for half in range(PS // 2):
        gathered = jnp.concatenate(
            [
                jnp.concatenate(
                    [
                        part[j * groups:(j + 1) * groups, half * pair:(half + 1) * pair]
                        for j in range(PS)
                    ],
                    axis=1,
                )
                for part in columns
            ],
            axis=0,
        )
        width = PS * pair
        raster[
            pl.ds(pl.multiple_of(block * patches * groups, patches * groups), patches * groups),
            half * width:(half + 1) * width,
        ] = dot(gathered, spread_ref[...]).astype(BF16)

    @pl.when(step == steps - 1)
    def _():
        count = raster.shape[0]
        slots = 256
        tokens = raster[...]
        for first in range(0, count, slots):
            slot = lax.broadcasted_iota(jnp.int32, (slots, count), 0) + first
            chosen_token = jnp.where(slot == place_ref[...], 1.0, 0.0).astype(BF16)
            tokens_ref[first:first + slots, :] = dot(chosen_token, tokens).astype(BF16)


def project(pixels, halo, valid, projector, offset, place, spread):
    local_rows, bands, cols = pixels.shape
    comps = projector.shape[0]
    steps = local_rows // STEP
    patch_count = (local_rows // PS) * (cols // PS)
    width = PS * PS * comps
    return pl.pallas_call(
        project_kernel,
        grid=(steps,),
        in_specs=[
            pl.BlockSpec((STEP, bands, cols), lambda i: (steps - 1 - i, 0, 0)),
            pl.BlockSpec((1, bands, cols), lambda i: (0, 0, 0)),
            pl.BlockSpec(memory_space=pltpu.SMEM),
            pl.BlockSpec(projector.shape, lambda i: (0, 0)),
            pl.BlockSpec(offset.shape, lambda i: (0, 0)),
            pl.BlockSpec(place.shape, lambda i: (0, 0)),
            pl.BlockSpec(spread.shape, lambda i: (0, 0)),
        ],
        out_specs=[
            pl.BlockSpec((patch_count, width), lambda i: (0, 0)),
            pl.BlockSpec((STEP, comps, cols), lambda i: (steps - 1 - i, 0, 0)),
        ],
        out_shape=[
            jax.ShapeDtypeStruct((patch_count, width), BF16),
            jax.ShapeDtypeStruct((local_rows, comps, cols), BF16),
        ],
        scratch_shapes=[
            pltpu.VMEM((comps, cols), F32),
            pltpu.VMEM((patch_count, width), BF16),
        ],
        compiler_params=pltpu.CompilerParams(vmem_limit_bytes=48 * 2**20),
        name="project",
    )(pixels, halo, valid, projector, offset, place, spread)


def local(pixels, scene_starts, owners, start_basis):
    row_count = lax.axis_size("rows")
    local_rows, bands, local_cols = pixels.shape
    total_rows = local_rows * row_count
    total_cols = local_cols * lax.axis_size("tok")
    scenes = scene_starts.shape[0]
    comps = start_basis.shape[1]
    halo = passed_along(pixels[0:1], "rows", -1)
    global_row = lax.axis_index("rows") * local_rows + jnp.arange(local_rows, dtype=jnp.int32)
    successor = global_row + 1
    starting = jnp.any(successor[:, None] == scene_starts[None, :], axis=1)
    valid = jnp.logical_and(successor < total_rows, jnp.logical_not(starting)).astype(jnp.int32)
    noise_norm = float(2 * (total_rows - scenes) * total_cols)
    pixel_total = float(total_rows * total_cols)
    sums = lax.psum(moments(pixels, halo, valid), ("rows", "tok"))
    projector, offset = make_projector(*sums, start_basis.T, noise_norm, pixel_total)

    patch_owner = owners.reshape(-1)
    patch_count = patch_owner.shape[0]
    per_owner = patch_count // row_count
    index = jnp.arange(patch_count, dtype=jnp.int32)
    matches = (patch_owner[None, :] == jnp.arange(row_count, dtype=jnp.int32)[:, None])
    earlier = (index[:, None] < index[None, :]).astype(BF16)
    running = jnp.dot(matches.astype(BF16), earlier, preferred_element_type=F32)
    rank = jnp.sum(jnp.where(matches, running, 0.0), axis=0).astype(jnp.int32)
    place = (patch_owner * per_owner + rank)[None, :]
    source = jnp.arange(2 * comps * PS, dtype=jnp.int32)
    j, within = source // (2 * comps), source % (2 * comps)
    target = (within // comps) * (PS * comps) + j * comps + within % comps
    spread = (target[:, None] == source[None, :]).astype(BF16)

    outgoing, noise_scores = project(pixels, halo, valid, projector, offset, place, spread)
    outgoing = outgoing.reshape(row_count, per_owner, -1)
    arrived = lax.all_to_all(outgoing, "rows", split_axis=0, concat_axis=0, tiled=True)
    return (arrived.reshape(patch_count, -1), noise_scores)


def solution(mesh):
    placed = (P("rows", None, "tok"), P(), P("rows", "tok"), P())
    return jax.shard_map(
        local,
        mesh=mesh,
        in_specs=placed,
        out_specs=(P(("rows", "tok"), None), P("rows", None, "tok")),
        check_vma=False,
    )
```

```python
import functools

import jax
import jax.numpy as jnp
from jax import lax
from jax.experimental import pallas as pl
from jax.experimental.pallas import tpu as pltpu
from jax.sharding import PartitionSpec as P

PS = 4
NS_ITERS = 10
STEP = 16
HALF = 256
F32 = jnp.float32
BF16 = jnp.bfloat16
NT = (((1,), (1,)), ((), ()))


def up(value, unit):
    return -(-value // unit) * unit


def passed_along(value, axis, steps):
    count = lax.axis_size(axis)
    leading, last = (max(0, -steps), min(count, count - steps))
    return lax.ppermute(value, axis, [(source, source + steps) for source in range(leading, last)])


def moments_kernel(x_ref, ahead_ref, halo_ref, valid_ref, wide_ref, tail_ref, band_ref, xs, ds, total):
    step = pl.program_id(0)
    steps = pl.num_programs(0)
    rows, bands, cols = x_ref.shape
    tall = xs.shape[0]

    @pl.when(step == 0)
    def _():
        wide_ref[...] = jnp.zeros_like(wide_ref)
        tail_ref[...] = jnp.zeros_like(tail_ref)
        total[...] = jnp.zeros_like(total)
        xs[...] = jnp.zeros_like(xs)
        ds[...] = jnp.zeros_like(ds)

    last = step == steps - 1
    here = x_ref[0].astype(F32)
    sums = total[...]
    for r in range(rows):
        if r + 1 < rows:
            after = x_ref[r + 1].astype(F32)
        else:
            after = jnp.where(last, halo_ref[0], ahead_ref[0]).astype(F32)
        keep = valid_ref[step * rows + r] != 0
        at = slice(r * cols, (r + 1) * cols)
        xs[0:bands, at] = x_ref[r]
        ds[0:bands, at] = jnp.where(keep, here - after, 0.0).astype(BF16)
        sums = sums + here
        here = after
    total[...] = sums
    for index, ref in enumerate((ds, xs)):
        wide_ref[index] += lax.dot_general(
            ref[...], ref[0:HALF, :], NT, preferred_element_type=F32
        )
        tail_ref[index] += lax.dot_general(
            ref[HALF:tall, :], ref[HALF:tall, :], NT, preferred_element_type=F32
        )

    @pl.when(last)
    def _():
        band_ref[...] = jnp.zeros_like(band_ref)
        band_ref[0:bands, :] = jnp.sum(total[...], axis=1, keepdims=True)


def moments(pixels, halo, valid):
    local_rows, bands, cols = pixels.shape
    tall = up(bands, 16)
    steps = local_rows // STEP
    last_row = local_rows - 1
    return pl.pallas_call(
        moments_kernel,
        grid=(steps,),
        in_specs=[
            pl.BlockSpec((STEP, bands, cols), lambda i: (i, 0, 0)),
            pl.BlockSpec((1, bands, cols), lambda i: (jnp.minimum((i + 1) * STEP, last_row), 0, 0)),
            pl.BlockSpec((1, bands, cols), lambda i: (0, 0, 0)),
            pl.BlockSpec(memory_space=pltpu.SMEM),
        ],
        out_specs=[
            pl.BlockSpec((2, tall, HALF), lambda i: (0, 0, 0)),
            pl.BlockSpec((2, tall - HALF, tall - HALF), lambda i: (0, 0, 0)),
            pl.BlockSpec((tall, 1), lambda i: (0, 0)),
        ],
        out_shape=[
            jax.ShapeDtypeStruct((2, tall, HALF), F32),
            jax.ShapeDtypeStruct((2, tall - HALF, tall - HALF), F32),
            jax.ShapeDtypeStruct((tall, 1), F32),
        ],
        scratch_shapes=[
            pltpu.VMEM((tall, STEP * cols), BF16),
            pltpu.VMEM((tall, STEP * cols), BF16),
            pltpu.VMEM((bands, cols), F32),
        ],
        compiler_params=pltpu.CompilerParams(vmem_limit_bytes=48 * 2**20),
        cost_estimate=pl.CostEstimate(
            flops=4 * local_rows * cols * bands * bands,
            bytes_accessed=2 * local_rows * cols * bands,
            transcendentals=0,
        ),
        name="moments",
    )(pixels, pixels, halo, valid)


def exchanges():
    plan = []
    for axis in ("rows", "tok"):
        bit = 1
        while bit < lax.axis_size(axis):
            plan.append((axis, bit))
            bit *= 2
    return plan


def total_kernel(plan, mine_ref, total_ref, held, gathered, *rest):
    count = len(plan)
    landing, (send_sem, recv_sem) = rest[:count], rest[count:]
    partners, bits = [], []
    for axis, bit in plan:
        index = lax.axis_index(axis)
        side = lax.rem(lax.div(index, bit), 2)
        bits.append(side)
        place = {"rows": lax.axis_index("rows"), "tok": lax.axis_index("tok")}
        place[axis] = index + bit * (1 - 2 * side)
        partners.append((place["rows"], place["tok"]))

    barrier = pltpu.get_barrier_semaphore()
    for partner in partners:
        pl.semaphore_signal(
            barrier, inc=1, device_id=partner, device_id_type=pl.DeviceIdType.MESH
        )
    pl.semaphore_wait(barrier, count)

    held[...] = mine_ref[...]
    base, length = 0, held.shape[0]
    regions = []
    for step in range(count):
        length //= 2
        keep = pl.multiple_of(base + bits[step] * length, 8)
        give = pl.multiple_of(base + (1 - bits[step]) * length, 8)
        copy = pltpu.make_async_remote_copy(
            src_ref=held.at[pl.ds(give, length)],
            dst_ref=landing[step],
            send_sem=send_sem.at[step],
            recv_sem=recv_sem.at[step],
            device_id=partners[step],
            device_id_type=pl.DeviceIdType.MESH,
        )
        copy.start()
        copy.wait()
        held[pl.ds(keep, length), :] += landing[step][...]
        regions.append((keep, length))
        base = keep
    gathered[pl.ds(base, length), :] = held[pl.ds(base, length), :]
    for step in reversed(range(count)):
        keep, length = regions[step]
        copy = pltpu.make_async_remote_copy(
            src_ref=gathered.at[pl.ds(keep, length)],
            dst_ref=gathered.at[pl.ds(keep, length)],
            send_sem=send_sem.at[count + step],
            recv_sem=recv_sem.at[count + step],
            device_id=partners[step],
            device_id_type=pl.DeviceIdType.MESH,
        )
        copy.start()
        copy.wait()
    total_ref[...] = gathered[...]


def summed(wide, tail, band):
    plan = exchanges()
    devices = 2 ** len(plan)
    tall, half = wide.shape[1:]
    short = tail.shape[1]
    flat = jnp.concatenate(
        [
            wide.reshape(2 * tall, half),
            jnp.pad(tail.reshape(2 * short, short), ((0, 0), (0, half - short))),
            jnp.pad(band.reshape(-1), (0, up(tall, half) - tall)).reshape(-1, half),
        ],
        axis=0,
    )
    rows = flat.shape[0]
    full = up(rows, 8 * devices)
    flat = jnp.pad(flat, ((0, full - rows), (0, 0)))
    landing = [pltpu.VMEM((full >> (step + 1), half), F32) for step in range(len(plan))]
    whole = pl.pallas_call(
        functools.partial(total_kernel, plan),
        out_shape=jax.ShapeDtypeStruct((full, half), F32),
        in_specs=[pl.BlockSpec(memory_space=pltpu.VMEM)],
        out_specs=pl.BlockSpec(memory_space=pltpu.VMEM),
        scratch_shapes=[pltpu.VMEM((full, half), F32), pltpu.VMEM((full, half), F32)]
        + landing
        + [pltpu.SemaphoreType.DMA((2 * len(plan),)), pltpu.SemaphoreType.DMA((2 * len(plan),))],
        compiler_params=pltpu.CompilerParams(
            collective_id=0, has_side_effects=True, vmem_limit_bytes=32 * 2**20
        ),
        name="total",
    )(flat)
    first, second = 2 * tall, 2 * tall + 2 * short
    return (
        whole[:first].reshape(2, tall, half),
        whole[first:second, :short].reshape(2, short, short),
        whole[second:rows].reshape(-1)[:tall].reshape(tall, 1),
    )


def split(value):
    high = value.astype(BF16)
    return high, (value - high.astype(F32)).astype(BF16)


def dot3(left, right):
    (lh, ll), (rh, rl) = left, right
    dot = functools.partial(jnp.dot, preferred_element_type=F32)
    return dot(lh, rh) + (dot(ll, rh) + dot(lh, rl))


def dot3_nt(left, right):
    (lh, ll), (rh, rl) = left, right
    dot = functools.partial(lax.dot_general, dimension_numbers=NT, preferred_element_type=F32)
    return dot(lh, rh) + (dot(ll, rh) + dot(lh, rl))


def projector_kernel(
    noise_norm, pixel_total, wide_ref, tail_ref, band_ref, start_ref, proj_ref, offset_ref,
    full, uh, ul, lh, ll, mh, ml, sh, sl,
):
    size = full.shape[0]
    tall = wide_ref.shape[1]
    bands = proj_ref.shape[1]
    comps = proj_ref.shape[0]
    rows = lax.broadcasted_iota(jnp.int32, (size, size), 0)
    lanes = lax.broadcasted_iota(jnp.int32, (size, size), 1)
    eye = jnp.where(rows == lanes, 1.0, 0.0).astype(F32)[0:tall]

    def assemble(index):
        full[...] = jnp.zeros_like(full)
        full[0:tall, 0:HALF] = wide_ref[index]
        full[HALF:tall, HALF:tall] = tail_ref[index]
        full[0:HALF, HALF:size] = full[HALF:size, 0:HALF].T
        return full[0:tall, :]

    def put(high, low, value):
        high[0:tall, :], low[0:tall, :] = split(value)

    for ref in (uh, ul, lh, ll, mh, ml, sh, sl):
        ref[...] = jnp.zeros_like(ref)
    band = jnp.broadcast_to(band_ref[...], (tall, 128)) / pixel_total
    band = jnp.concatenate([band, jnp.zeros((size - tall, 128), F32)], axis=0)
    mean_col = band[0:tall, 0:1]
    mean_row = band.T[0:1, :]
    put(sh, sl, assemble(1) / pixel_total - mean_col * mean_row)

    noise_cov = assemble(0) / noise_norm
    scale = jnp.max(jnp.sum(jnp.abs(noise_cov), axis=1, keepdims=True), axis=0, keepdims=True)
    upper = noise_cov / scale
    put(uh, ul, upper)
    middle = 1.5 * eye - 0.5 * upper
    put(mh, ml, middle)
    put(lh, ll, middle)

    def pair(high, low):
        return high[...], low[...]

    def left(high, low):
        return high[0:tall, :], low[0:tall, :]

    put(uh, ul, dot3(left(uh, ul), pair(mh, ml)))

    def iteration(repeat, carry):
        put(mh, ml, 1.5 * eye - 0.5 * dot3(left(lh, ll), pair(uh, ul)))
        put(uh, ul, dot3(left(uh, ul), pair(mh, ml)))
        put(lh, ll, dot3(left(lh, ll), pair(mh, ml)))
        return carry

    lax.fori_loop(0, NS_ITERS - 2, iteration, 0)
    put(mh, ml, 1.5 * eye - 0.5 * dot3(left(lh, ll), pair(uh, ul)))
    whitener = dot3(left(lh, ll), pair(mh, ml)) * lax.rsqrt(scale)
    put(lh, ll, whitener)

    def whitened(block):
        for high, low in ((lh, ll), (sh, sl), (lh, ll)):
            block = dot3(split(block), pair(high, low))
        return block

    block = whitened(start_ref[...])
    largest = jnp.max(jnp.max(jnp.abs(block), axis=1, keepdims=True), axis=0, keepdims=True)
    block = whitened(block / largest)
    largest = jnp.max(jnp.max(jnp.abs(block), axis=1, keepdims=True), axis=0, keepdims=True)
    block = block / largest
    gram = lax.dot_general(
        block, block, NT, precision=lax.Precision.HIGHEST, preferred_element_type=F32
    )
    k_rows = lax.broadcasted_iota(jnp.int32, (comps, comps), 0)
    k_lanes = lax.broadcasted_iota(jnp.int32, (comps, comps), 1)
    work = jnp.concatenate([gram, jnp.where(k_rows == k_lanes, 1.0, 0.0).astype(F32)], axis=1)
    row_index = lax.broadcasted_iota(jnp.int32, (comps, 2 * comps), 0)
    for j in range(comps):
        pivot_row = work[j:j + 1, :]
        inverse = lax.rsqrt(pivot_row[:, j:j + 1])
        pivot_row = pivot_row * inverse
        factor = work[:, j:j + 1] * inverse
        work = jnp.where(
            row_index > j, work - factor * pivot_row, jnp.where(row_index == j, pivot_row, work)
        )
    basis = jnp.dot(
        work[:, comps:], block, precision=lax.Precision.HIGHEST, preferred_element_type=F32
    )
    projector = dot3(split(basis), pair(lh, ll)).astype(BF16)
    proj_ref[...] = projector[:, 0:bands]
    offset = jnp.sum(projector.astype(F32) * mean_row, axis=1, keepdims=True)
    offset_ref[...] = jnp.broadcast_to(offset, offset_ref.shape)


def make_projector(wide, tail, band, start, noise_norm, pixel_total):
    tall = wide.shape[1]
    comps, size = start.shape[0], up(tall, 128)
    square = pltpu.VMEM((size, size), BF16)
    return pl.pallas_call(
        functools.partial(projector_kernel, noise_norm, pixel_total),
        out_shape=[
            jax.ShapeDtypeStruct((comps, tall), BF16),
            jax.ShapeDtypeStruct((comps, 128), F32),
        ],
        scratch_shapes=[pltpu.VMEM((size, size), F32)] + [square] * 8,
        compiler_params=pltpu.CompilerParams(vmem_limit_bytes=48 * 2**20),
        name="projector",
    )(wide, tail, band, jnp.pad(start, ((0, 0), (0, size - start.shape[1]))))


def project_kernel(
    x_ref, halo_ref, valid_ref, proj_ref, offset_ref, place_ref, spread_ref,
    tokens_ref, scores_ref, ahead, raster,
):
    step = pl.program_id(0)
    steps = pl.num_programs(0)
    block = steps - 1 - step
    rows, bands, cols = x_ref.shape
    comps = proj_ref.shape[0]
    projector = proj_ref[...][:, 0:bands]
    dot = functools.partial(jnp.dot, preferred_element_type=F32)

    @pl.when(step == 0)
    def _():
        ahead[...] = dot(projector, halo_ref[0])

    pixels = jnp.concatenate([x_ref[r] for r in range(rows)], axis=1)
    sums = dot(projector, pixels)
    offset = offset_ref[...]
    after = ahead[...]
    for r in reversed(range(rows)):
        here = sums[:, r * cols:(r + 1) * cols]
        keep = valid_ref[block * rows + r] != 0
        scores_ref[r] = jnp.where(keep, here - after, 0.0).astype(BF16)
        after = here
    ahead[...] = after

    patches = rows // PS
    groups = cols // PS
    chosen_row = lax.broadcasted_iota(jnp.int32, (cols, cols), 0)
    chosen_col = lax.broadcasted_iota(jnp.int32, (cols, cols), 1)
    chosen = jnp.where(
        chosen_col == PS * lax.rem(chosen_row, groups) + lax.div(chosen_row, groups), 1.0, 0.0
    ).astype(BF16)
    columns = []
    for p in range(patches):
        parts = []
        for i in range(PS):
            r = p * PS + i
            parts.append((sums[:, r * cols:(r + 1) * cols] - offset).astype(BF16))
        stacked = jnp.concatenate(parts, axis=0)
        columns.append(
            lax.dot_general(chosen, stacked, NT, preferred_element_type=F32).astype(BF16)
        )
    pair = 2 * comps
    for half in range(PS // 2):
        gathered = jnp.concatenate(
            [
                jnp.concatenate(
                    [
                        part[j * groups:(j + 1) * groups, half * pair:(half + 1) * pair]
                        for j in range(PS)
                    ],
                    axis=1,
                )
                for part in columns
            ],
            axis=0,
        )
        width = PS * pair
        raster[
            pl.ds(pl.multiple_of(block * patches * groups, patches * groups), patches * groups),
            half * width:(half + 1) * width,
        ] = dot(gathered, spread_ref[...]).astype(BF16)

    @pl.when(step == steps - 1)
    def _():
        count = raster.shape[0]
        slots = 256
        tokens = raster[...]
        for first in range(0, count, slots):
            slot = lax.broadcasted_iota(jnp.int32, (slots, count), 0) + first
            chosen_token = jnp.where(slot == place_ref[...], 1.0, 0.0).astype(BF16)
            tokens_ref[first:first + slots, :] = dot(chosen_token, tokens).astype(BF16)


def project(pixels, halo, valid, projector, offset, place, spread):
    local_rows, bands, cols = pixels.shape
    comps = projector.shape[0]
    steps = local_rows // STEP
    patch_count = (local_rows // PS) * (cols // PS)
    width = PS * PS * comps
    return pl.pallas_call(
        project_kernel,
        grid=(steps,),
        in_specs=[
            pl.BlockSpec((STEP, bands, cols), lambda i: (steps - 1 - i, 0, 0)),
            pl.BlockSpec((1, bands, cols), lambda i: (0, 0, 0)),
            pl.BlockSpec(memory_space=pltpu.SMEM),
            pl.BlockSpec(projector.shape, lambda i: (0, 0)),
            pl.BlockSpec(offset.shape, lambda i: (0, 0)),
            pl.BlockSpec(place.shape, lambda i: (0, 0)),
            pl.BlockSpec(spread.shape, lambda i: (0, 0)),
        ],
        out_specs=[
            pl.BlockSpec((patch_count, width), lambda i: (0, 0)),
            pl.BlockSpec((STEP, comps, cols), lambda i: (steps - 1 - i, 0, 0)),
        ],
        out_shape=[
            jax.ShapeDtypeStruct((patch_count, width), BF16),
            jax.ShapeDtypeStruct((local_rows, comps, cols), BF16),
        ],
        scratch_shapes=[
            pltpu.VMEM((comps, cols), F32),
            pltpu.VMEM((patch_count, width), BF16),
        ],
        compiler_params=pltpu.CompilerParams(vmem_limit_bytes=48 * 2**20),
        name="project",
    )(pixels, halo, valid, projector, offset, place, spread)


def local(pixels, scene_starts, owners, start_basis):
    row_count = lax.axis_size("rows")
    local_rows, bands, local_cols = pixels.shape
    total_rows = local_rows * row_count
    total_cols = local_cols * lax.axis_size("tok")
    scenes = scene_starts.shape[0]
    comps = start_basis.shape[1]
    halo = passed_along(pixels[0:1], "rows", -1)
    global_row = lax.axis_index("rows") * local_rows + jnp.arange(local_rows, dtype=jnp.int32)
    successor = global_row + 1
    starting = jnp.any(successor[:, None] == scene_starts[None, :], axis=1)
    valid = jnp.logical_and(successor < total_rows, jnp.logical_not(starting)).astype(jnp.int32)
    noise_norm = float(2 * (total_rows - scenes) * total_cols)
    pixel_total = float(total_rows * total_cols)
    sums = summed(*moments(pixels, halo, valid))
    projector, offset = make_projector(*sums, start_basis.T, noise_norm, pixel_total)

    patch_owner = owners.reshape(-1)
    patch_count = patch_owner.shape[0]
    per_owner = patch_count // row_count
    index = jnp.arange(patch_count, dtype=jnp.int32)
    matches = (patch_owner[None, :] == jnp.arange(row_count, dtype=jnp.int32)[:, None])
    earlier = (index[:, None] < index[None, :]).astype(BF16)
    running = jnp.dot(matches.astype(BF16), earlier, preferred_element_type=F32)
    rank = jnp.sum(jnp.where(matches, running, 0.0), axis=0).astype(jnp.int32)
    place = (patch_owner * per_owner + rank)[None, :]
    source = jnp.arange(2 * comps * PS, dtype=jnp.int32)
    j, within = source // (2 * comps), source % (2 * comps)
    target = (within // comps) * (PS * comps) + j * comps + within % comps
    spread = (target[:, None] == source[None, :]).astype(BF16)

    outgoing, noise_scores = project(pixels, halo, valid, projector, offset, place, spread)
    outgoing = outgoing.reshape(row_count, per_owner, -1)
    arrived = lax.all_to_all(outgoing, "rows", split_axis=0, concat_axis=0, tiled=True)
    return (arrived.reshape(patch_count, -1), noise_scores)


def solution(mesh):
    placed = (P("rows", None, "tok"), P(), P("rows", "tok"), P())
    return jax.shard_map(
        local,
        mesh=mesh,
        in_specs=placed,
        out_specs=(P(("rows", "tok"), None), P("rows", None, "tok")),
        check_vma=False,
    )
```

```python
import functools

import jax
import jax.numpy as jnp
from jax import lax
from jax.experimental import pallas as pl
from jax.experimental.pallas import tpu as pltpu
from jax.sharding import PartitionSpec as P

PS = 4
NS_ITERS = 10
STEP = 16
HALF = 256
F32 = jnp.float32
BF16 = jnp.bfloat16
NT = (((1,), (1,)), ((), ()))


def up(value, unit):
    return -(-value // unit) * unit


def passed_along(value, axis, steps):
    count = lax.axis_size(axis)
    leading, last = (max(0, -steps), min(count, count - steps))
    return lax.ppermute(value, axis, [(source, source + steps) for source in range(leading, last)])


def moments_kernel(x_ref, ahead_ref, halo_ref, valid_ref, wide_ref, tail_ref, band_ref, xs, ds, total):
    step = pl.program_id(0)
    steps = pl.num_programs(0)
    rows, bands, cols = x_ref.shape
    tall = xs.shape[0]

    @pl.when(step == 0)
    def _():
        wide_ref[...] = jnp.zeros_like(wide_ref)
        tail_ref[...] = jnp.zeros_like(tail_ref)
        total[...] = jnp.zeros_like(total)
        xs[...] = jnp.zeros_like(xs)
        ds[...] = jnp.zeros_like(ds)

    last = step == steps - 1
    here = x_ref[0].astype(F32)
    sums = total[...]
    for r in range(rows):
        if r + 1 < rows:
            after = x_ref[r + 1].astype(F32)
        else:
            after = jnp.where(last, halo_ref[0], ahead_ref[0]).astype(F32)
        keep = valid_ref[step * rows + r] != 0
        at = slice(r * cols, (r + 1) * cols)
        xs[0:bands, at] = x_ref[r]
        ds[0:bands, at] = jnp.where(keep, here - after, 0.0).astype(BF16)
        sums = sums + here
        here = after
    total[...] = sums
    for index, ref in enumerate((ds, xs)):
        wide_ref[index] += lax.dot_general(
            ref[...], ref[0:HALF, :], NT, preferred_element_type=F32
        )
        tail_ref[index] += lax.dot_general(
            ref[HALF:tall, :], ref[HALF:tall, :], NT, preferred_element_type=F32
        )

    @pl.when(last)
    def _():
        band_ref[...] = jnp.zeros_like(band_ref)
        band_ref[0:bands, :] = jnp.sum(total[...], axis=1, keepdims=True)


def moments(pixels, halo, valid):
    local_rows, bands, cols = pixels.shape
    tall = up(bands, 16)
    steps = local_rows // STEP
    last_row = local_rows - 1
    return pl.pallas_call(
        moments_kernel,
        grid=(steps,),
        in_specs=[
            pl.BlockSpec((STEP, bands, cols), lambda i: (i, 0, 0)),
            pl.BlockSpec((1, bands, cols), lambda i: (jnp.minimum((i + 1) * STEP, last_row), 0, 0)),
            pl.BlockSpec((1, bands, cols), lambda i: (0, 0, 0)),
            pl.BlockSpec(memory_space=pltpu.SMEM),
        ],
        out_specs=[
            pl.BlockSpec((2, tall, HALF), lambda i: (0, 0, 0)),
            pl.BlockSpec((2, tall - HALF, tall - HALF), lambda i: (0, 0, 0)),
            pl.BlockSpec((tall, 1), lambda i: (0, 0)),
        ],
        out_shape=[
            jax.ShapeDtypeStruct((2, tall, HALF), F32),
            jax.ShapeDtypeStruct((2, tall - HALF, tall - HALF), F32),
            jax.ShapeDtypeStruct((tall, 1), F32),
        ],
        scratch_shapes=[
            pltpu.VMEM((tall, STEP * cols), BF16),
            pltpu.VMEM((tall, STEP * cols), BF16),
            pltpu.VMEM((bands, cols), F32),
        ],
        compiler_params=pltpu.CompilerParams(vmem_limit_bytes=58 * 2**20),
        cost_estimate=pl.CostEstimate(
            flops=4 * local_rows * cols * bands * bands,
            bytes_accessed=2 * local_rows * cols * bands,
            transcendentals=0,
        ),
        name="moments",
    )(pixels, pixels, halo, valid)


def exchanges():
    plan = []
    for axis in ("rows", "tok"):
        bit = 1
        while bit < lax.axis_size(axis):
            plan.append((axis, bit))
            bit *= 2
    return plan


def total_kernel(plan, mine_ref, total_ref, held, gathered, *rest):
    count = len(plan)
    landing, (send_sem, recv_sem) = rest[:count], rest[count:]
    partners, bits = [], []
    for axis, bit in plan:
        index = lax.axis_index(axis)
        side = lax.rem(lax.div(index, bit), 2)
        bits.append(side)
        place = {"rows": lax.axis_index("rows"), "tok": lax.axis_index("tok")}
        place[axis] = index + bit * (1 - 2 * side)
        partners.append((place["rows"], place["tok"]))

    barrier = pltpu.get_barrier_semaphore()
    for partner in partners:
        pl.semaphore_signal(
            barrier, inc=1, device_id=partner, device_id_type=pl.DeviceIdType.MESH
        )
    pl.semaphore_wait(barrier, count)

    held[...] = mine_ref[...]
    base, length = 0, held.shape[0]
    regions = []
    for step in range(count):
        length //= 2
        keep = pl.multiple_of(base + bits[step] * length, 8)
        give = pl.multiple_of(base + (1 - bits[step]) * length, 8)
        copy = pltpu.make_async_remote_copy(
            src_ref=held.at[pl.ds(give, length)],
            dst_ref=landing[step],
            send_sem=send_sem.at[step],
            recv_sem=recv_sem.at[step],
            device_id=partners[step],
            device_id_type=pl.DeviceIdType.MESH,
        )
        copy.start()
        copy.wait()
        held[pl.ds(keep, length), :] += landing[step][...]
        regions.append((keep, length))
        base = keep
    gathered[pl.ds(base, length), :] = held[pl.ds(base, length), :]
    for step in reversed(range(count)):
        keep, length = regions[step]
        copy = pltpu.make_async_remote_copy(
            src_ref=gathered.at[pl.ds(keep, length)],
            dst_ref=gathered.at[pl.ds(keep, length)],
            send_sem=send_sem.at[count + step],
            recv_sem=recv_sem.at[count + step],
            device_id=partners[step],
            device_id_type=pl.DeviceIdType.MESH,
        )
        copy.start()
        copy.wait()
    total_ref[...] = gathered[...]


def summed(wide, tail, band):
    plan = exchanges()
    devices = 2 ** len(plan)
    tall, half = wide.shape[1:]
    short = tail.shape[1]
    flat = jnp.concatenate(
        [
            wide.reshape(2 * tall, half),
            jnp.pad(tail.reshape(2 * short, short), ((0, 0), (0, half - short))),
            jnp.pad(band.reshape(-1), (0, up(tall, half) - tall)).reshape(-1, half),
        ],
        axis=0,
    )
    rows = flat.shape[0]
    full = up(rows, 8 * devices)
    flat = jnp.pad(flat, ((0, full - rows), (0, 0)))
    landing = [pltpu.VMEM((full >> (step + 1), half), F32) for step in range(len(plan))]
    whole = pl.pallas_call(
        functools.partial(total_kernel, plan),
        out_shape=jax.ShapeDtypeStruct((full, half), F32),
        in_specs=[pl.BlockSpec(memory_space=pltpu.VMEM)],
        out_specs=pl.BlockSpec(memory_space=pltpu.VMEM),
        scratch_shapes=[pltpu.VMEM((full, half), F32), pltpu.VMEM((full, half), F32)]
        + landing
        + [pltpu.SemaphoreType.DMA((2 * len(plan),)), pltpu.SemaphoreType.DMA((2 * len(plan),))],
        compiler_params=pltpu.CompilerParams(
            collective_id=0, has_side_effects=True, vmem_limit_bytes=32 * 2**20
        ),
        name="total",
    )(flat)
    first, second = 2 * tall, 2 * tall + 2 * short
    return (
        whole[:first].reshape(2, tall, half),
        whole[first:second, :short].reshape(2, short, short),
        whole[second:rows].reshape(-1)[:tall].reshape(tall, 1),
    )


def split(value):
    high = value.astype(BF16)
    return high, (value - high.astype(F32)).astype(BF16)


def dot3(left, right):
    (lh, ll), (rh, rl) = left, right
    dot = functools.partial(jnp.dot, preferred_element_type=F32)
    return dot(lh, rh) + (dot(ll, rh) + dot(lh, rl))


def dot3_nt(left, right):
    (lh, ll), (rh, rl) = left, right
    dot = functools.partial(lax.dot_general, dimension_numbers=NT, preferred_element_type=F32)
    return dot(lh, rh) + (dot(ll, rh) + dot(lh, rl))


def projector_kernel(
    noise_norm, pixel_total, wide_ref, tail_ref, band_ref, start_ref, proj_ref, offset_ref,
    full, uh, ul, lh, ll, mh, ml, sh, sl,
):
    size = full.shape[0]
    tall = wide_ref.shape[1]
    bands = proj_ref.shape[1]
    comps = proj_ref.shape[0]
    rows = lax.broadcasted_iota(jnp.int32, (size, size), 0)
    lanes = lax.broadcasted_iota(jnp.int32, (size, size), 1)
    eye = jnp.where(rows == lanes, 1.0, 0.0).astype(F32)[0:tall]

    def assemble(index):
        full[...] = jnp.zeros_like(full)
        full[0:tall, 0:HALF] = wide_ref[index]
        full[HALF:tall, HALF:tall] = tail_ref[index]
        full[0:HALF, HALF:size] = full[HALF:size, 0:HALF].T
        return full[0:tall, :]

    def put(high, low, value):
        high[0:tall, :], low[0:tall, :] = split(value)

    for ref in (uh, ul, lh, ll, mh, ml, sh, sl):
        ref[...] = jnp.zeros_like(ref)
    band = jnp.broadcast_to(band_ref[...], (tall, 128)) / pixel_total
    band = jnp.concatenate([band, jnp.zeros((size - tall, 128), F32)], axis=0)
    mean_col = band[0:tall, 0:1]
    mean_row = band.T[0:1, :]
    put(sh, sl, assemble(1) / pixel_total - mean_col * mean_row)

    noise_cov = assemble(0) / noise_norm
    scale = jnp.max(jnp.sum(jnp.abs(noise_cov), axis=1, keepdims=True), axis=0, keepdims=True)
    upper = noise_cov / scale
    put(uh, ul, upper)
    middle = 1.5 * eye - 0.5 * upper
    put(mh, ml, middle)
    put(lh, ll, middle)

    def pair(high, low):
        return high[...], low[...]

    def left(high, low):
        return high[0:tall, :], low[0:tall, :]

    put(uh, ul, dot3(left(uh, ul), pair(mh, ml)))

    def iteration(repeat, carry):
        put(mh, ml, 1.5 * eye - 0.5 * dot3(left(lh, ll), pair(uh, ul)))
        put(uh, ul, dot3(left(uh, ul), pair(mh, ml)))
        put(lh, ll, dot3(left(lh, ll), pair(mh, ml)))
        return carry

    lax.fori_loop(0, NS_ITERS - 2, iteration, 0)
    put(mh, ml, 1.5 * eye - 0.5 * dot3(left(lh, ll), pair(uh, ul)))
    whitener = dot3(left(lh, ll), pair(mh, ml)) * lax.rsqrt(scale)
    put(lh, ll, whitener)

    def whitened(block):
        for high, low in ((lh, ll), (sh, sl), (lh, ll)):
            block = dot3(split(block), pair(high, low))
        return block

    block = whitened(start_ref[...])
    largest = jnp.max(jnp.max(jnp.abs(block), axis=1, keepdims=True), axis=0, keepdims=True)
    block = whitened(block / largest)
    largest = jnp.max(jnp.max(jnp.abs(block), axis=1, keepdims=True), axis=0, keepdims=True)
    block = block / largest
    gram = lax.dot_general(
        block, block, NT, precision=lax.Precision.HIGHEST, preferred_element_type=F32
    )
    k_rows = lax.broadcasted_iota(jnp.int32, (comps, comps), 0)
    k_lanes = lax.broadcasted_iota(jnp.int32, (comps, comps), 1)
    work = jnp.concatenate([gram, jnp.where(k_rows == k_lanes, 1.0, 0.0).astype(F32)], axis=1)
    row_index = lax.broadcasted_iota(jnp.int32, (comps, 2 * comps), 0)
    for j in range(comps):
        pivot_row = work[j:j + 1, :]
        inverse = lax.rsqrt(pivot_row[:, j:j + 1])
        pivot_row = pivot_row * inverse
        factor = work[:, j:j + 1] * inverse
        work = jnp.where(
            row_index > j, work - factor * pivot_row, jnp.where(row_index == j, pivot_row, work)
        )
    basis = jnp.dot(
        work[:, comps:], block, precision=lax.Precision.HIGHEST, preferred_element_type=F32
    )
    projector = dot3(split(basis), pair(lh, ll)).astype(BF16)
    proj_ref[...] = projector[:, 0:bands]
    offset = jnp.sum(projector.astype(F32) * mean_row, axis=1, keepdims=True)
    offset_ref[...] = jnp.broadcast_to(offset, offset_ref.shape)


def make_projector(wide, tail, band, start, noise_norm, pixel_total):
    tall = wide.shape[1]
    comps, size = start.shape[0], up(tall, 128)
    square = pltpu.VMEM((size, size), BF16)
    return pl.pallas_call(
        functools.partial(projector_kernel, noise_norm, pixel_total),
        out_shape=[
            jax.ShapeDtypeStruct((comps, tall), BF16),
            jax.ShapeDtypeStruct((comps, 128), F32),
        ],
        scratch_shapes=[pltpu.VMEM((size, size), F32)] + [square] * 8,
        compiler_params=pltpu.CompilerParams(vmem_limit_bytes=58 * 2**20),
        name="projector",
    )(wide, tail, band, jnp.pad(start, ((0, 0), (0, size - start.shape[1]))))


def project_kernel(
    x_ref, halo_ref, valid_ref, proj_ref, offset_ref, place_ref, spread_ref,
    tokens_ref, scores_ref, ahead, raster,
):
    step = pl.program_id(0)
    steps = pl.num_programs(0)
    block = steps - 1 - step
    rows, bands, cols = x_ref.shape
    comps = proj_ref.shape[0]
    projector = proj_ref[...][:, 0:bands]
    dot = functools.partial(jnp.dot, preferred_element_type=F32)

    @pl.when(step == 0)
    def _():
        ahead[...] = dot(projector, halo_ref[0])

    pixels = jnp.concatenate([x_ref[r] for r in range(rows)], axis=1)
    sums = dot(projector, pixels)
    offset = offset_ref[...]
    after = ahead[...]
    for r in reversed(range(rows)):
        here = sums[:, r * cols:(r + 1) * cols]
        keep = valid_ref[block * rows + r] != 0
        scores_ref[r] = jnp.where(keep, here - after, 0.0).astype(BF16)
        after = here
    ahead[...] = after

    patches = rows // PS
    groups = cols // PS
    chosen_row = lax.broadcasted_iota(jnp.int32, (cols, cols), 0)
    chosen_col = lax.broadcasted_iota(jnp.int32, (cols, cols), 1)
    chosen = jnp.where(
        chosen_col == PS * lax.rem(chosen_row, groups) + lax.div(chosen_row, groups), 1.0, 0.0
    ).astype(BF16)
    columns = []
    for p in range(patches):
        parts = []
        for i in range(PS):
            r = p * PS + i
            parts.append((sums[:, r * cols:(r + 1) * cols] - offset).astype(BF16))
        stacked = jnp.concatenate(parts, axis=0)
        columns.append(
            lax.dot_general(chosen, stacked, NT, preferred_element_type=F32).astype(BF16)
        )
    pair = 2 * comps
    for half in range(PS // 2):
        gathered = jnp.concatenate(
            [
                jnp.concatenate(
                    [
                        part[j * groups:(j + 1) * groups, half * pair:(half + 1) * pair]
                        for j in range(PS)
                    ],
                    axis=1,
                )
                for part in columns
            ],
            axis=0,
        )
        width = PS * pair
        raster[
            pl.ds(pl.multiple_of(block * patches * groups, patches * groups), patches * groups),
            half * width:(half + 1) * width,
        ] = dot(gathered, spread_ref[...]).astype(BF16)

    @pl.when(step == steps - 1)
    def _():
        count = raster.shape[0]
        slots = 256
        tokens = raster[...]
        for first in range(0, count, slots):
            slot = lax.broadcasted_iota(jnp.int32, (slots, count), 0) + first
            chosen_token = jnp.where(slot == place_ref[...], 1.0, 0.0).astype(BF16)
            tokens_ref[first:first + slots, :] = dot(chosen_token, tokens).astype(BF16)


def project(pixels, halo, valid, projector, offset, place, spread):
    local_rows, bands, cols = pixels.shape
    comps = projector.shape[0]
    steps = local_rows // STEP
    patch_count = (local_rows // PS) * (cols // PS)
    width = PS * PS * comps
    return pl.pallas_call(
        project_kernel,
        grid=(steps,),
        in_specs=[
            pl.BlockSpec((STEP, bands, cols), lambda i: (steps - 1 - i, 0, 0)),
            pl.BlockSpec((1, bands, cols), lambda i: (0, 0, 0)),
            pl.BlockSpec(memory_space=pltpu.SMEM),
            pl.BlockSpec(projector.shape, lambda i: (0, 0)),
            pl.BlockSpec(offset.shape, lambda i: (0, 0)),
            pl.BlockSpec(place.shape, lambda i: (0, 0)),
            pl.BlockSpec(spread.shape, lambda i: (0, 0)),
        ],
        out_specs=[
            pl.BlockSpec((patch_count, width), lambda i: (0, 0)),
            pl.BlockSpec((STEP, comps, cols), lambda i: (steps - 1 - i, 0, 0)),
        ],
        out_shape=[
            jax.ShapeDtypeStruct((patch_count, width), BF16),
            jax.ShapeDtypeStruct((local_rows, comps, cols), BF16),
        ],
        scratch_shapes=[
            pltpu.VMEM((comps, cols), F32),
            pltpu.VMEM((patch_count, width), BF16),
        ],
        compiler_params=pltpu.CompilerParams(vmem_limit_bytes=58 * 2**20),
        name="project",
    )(pixels, halo, valid, projector, offset, place, spread)


def local(pixels, scene_starts, owners, start_basis):
    row_count = lax.axis_size("rows")
    local_rows, bands, local_cols = pixels.shape
    total_rows = local_rows * row_count
    total_cols = local_cols * lax.axis_size("tok")
    scenes = scene_starts.shape[0]
    comps = start_basis.shape[1]
    halo = passed_along(pixels[0:1], "rows", -1)
    global_row = lax.axis_index("rows") * local_rows + jnp.arange(local_rows, dtype=jnp.int32)
    successor = global_row + 1
    starting = jnp.any(successor[:, None] == scene_starts[None, :], axis=1)
    valid = jnp.logical_and(successor < total_rows, jnp.logical_not(starting)).astype(jnp.int32)
    noise_norm = float(2 * (total_rows - scenes) * total_cols)
    pixel_total = float(total_rows * total_cols)
    sums = summed(*moments(pixels, halo, valid))
    projector, offset = make_projector(*sums, start_basis.T, noise_norm, pixel_total)

    patch_owner = owners.reshape(-1)
    patch_count = patch_owner.shape[0]
    per_owner = patch_count // row_count
    index = jnp.arange(patch_count, dtype=jnp.int32)
    matches = (patch_owner[None, :] == jnp.arange(row_count, dtype=jnp.int32)[:, None])
    earlier = (index[:, None] < index[None, :]).astype(BF16)
    running = jnp.dot(matches.astype(BF16), earlier, preferred_element_type=F32)
    rank = jnp.sum(jnp.where(matches, running, 0.0), axis=0).astype(jnp.int32)
    place = (patch_owner * per_owner + rank)[None, :]
    source = jnp.arange(2 * comps * PS, dtype=jnp.int32)
    j, within = source // (2 * comps), source % (2 * comps)
    target = (within // comps) * (PS * comps) + j * comps + within % comps
    spread = (target[:, None] == source[None, :]).astype(BF16)

    outgoing, noise_scores = project(pixels, halo, valid, projector, offset, place, spread)
    outgoing = outgoing.reshape(row_count, per_owner, -1)
    arrived = lax.all_to_all(outgoing, "rows", split_axis=0, concat_axis=0, tiled=True)
    return (arrived.reshape(patch_count, -1), noise_scores)


def solution(mesh):
    placed = (P("rows", None, "tok"), P(), P("rows", "tok"), P())
    return jax.shard_map(
        local,
        mesh=mesh,
        in_specs=placed,
        out_specs=(P(("rows", "tok"), None), P("rows", None, "tok")),
        check_vma=False,
    )
```
